512 devices in a mesh: section: 8 (over x, core), expert: 64 (over z, y).
Axes of the slice: x: 4, y: 4, z: 16, core: 2. Of those that a mesh axis runs over, the one named last changes fastest.
Arguments:
- fwd_sent: bfloat16 [8, 4096, 3584], P('section', 'expert'), may hold values from -6 to 6
- grad_sent: bfloat16 [8, 4096, 3584], P('section', 'expert'), may hold values from -6 to 6
- saved_scale: float32 [8, 4096], P('section', 'expert'), may hold values from 0.5 to 2
- norm_gain: float32 [8, 3584], P('section'), may hold values from 0.1 to 1.9
- w_in: bfloat16 [8, 64, 3584, 256], P('section', 'expert'), may hold values from -0.09375 to 0.09375
- w_down: bfloat16 [8, 64, 128, 3584], P('section', 'expert'), may hold values from -0.1875 to 0.1875
- saved_pre: bfloat16 [8, 64, 512, 256], P('section', 'expert'), may hold values from -5 to 5
- route_fwd: int32 [8, 4096, 1], P('section', 'expert'), may hold values from 0 to 7; in each aligned block of 64 rows (0 to 63, 64 to 127, ..., all dimensions but the last counted through in order) at most 8 rows name the same one
- route_bwd: int32 [8, 4096, 1], P('section', 'expert'), may hold values from 0 to 7; in each aligned block of 64 rows (0 to 63, 64 to 127, ..., all dimensions but the last counted through in order) at most 8 rows name the same one
- weight_fwd: float32 [8, 4096], P('section', 'expert'), may hold values from 0.2 to 1
- weight_bwd: float32 [8, 4096], P('section', 'expert'), may hold values from 0.2 to 1
Outputs:
- forward_out: bfloat16 [8, 4096, 3584], P('section', 'expert')
- backward_out: bfloat16 [8, 4096, 3584], P('section', 'expert')
The draws below stay inside these ranges and needn't reach their ends.
Inputs may be any that keep to these rules, and one draw needn't show every extreme that they name: `route_fwd`: in every layer, the 64 tokens of one aligned block route to each expert exactly 8 times. `route_bwd`: in every layer, the 64 tokens of one aligned block route to each expert exactly 8 times.
All inputs are finite; a program needn't handle non-finite values.
Results may differ from the reference program's by a relative error of at most 0.005.
Values may be sent and summed in bfloat16 or wider, within the bound.
No kernel may reach another device: no remote copies, remote signals or barrier semaphores. Data moves between devices by JAX's collectives and lax.ppermute only.
A program may use at most 64 MiB of HBM per device.

```python
import math
import jax
import jax.numpy as jnp
import numpy as np
from jax import lax

D = 3584
EXP_HIDDEN = 1024
EXPERTS = 8
TOP = 1
TOK_DEV = 64
CAP = 8
SPLIT = 8
H_DEV = 128
LAYERS = 8
TOKENS = 4096
N_EXPERT = 64


def shard_levels(key, dims, shards, least, high):
    gain = 1.0
    for dim, blocks in shards:
        steps = jax.random.uniform(jax.random.fold_in(jax.random.fold_in(key, 6), dim), (blocks,), jnp.float32, least / len(shards), high / len(shards))
        gain = gain * jnp.repeat(jnp.exp(steps), dims[dim] // blocks).reshape((-1,) + (1,) * (len(dims) - 1 - dim))
    return gain


def assign_block(rng, own, number, rows, count, top, most, skew):
    order = jax.random.permutation(rng, count)
    crowded, usual = load_shares(count, rows * top, most, skew, True), load_shares(count, rows * top, most, skew, False)
    places = jnp.arange(count)

    def named(tallies, turn):
        used = int((tallies > 0).sum())
        fixed = max(1, used // 4)
        moved = fixed + (places - fixed + turn * (used - fixed)) % max(1, count - fixed)
        return jnp.zeros((count,), jnp.int32).at[order[jnp.where(places < fixed, places, moved)]].set(jnp.asarray(tallies, jnp.int32))

    tallies = jnp.where(number % 4 == 0, named(crowded, number // 4), named(usual, number - number // 4 - 1))
    mixed = jax.random.permutation(jax.random.fold_in(own, 3), count)
    donor, receiver = mixed[0:count // 2 * 2:2], mixed[1:count // 2 * 2:2]
    room = jnp.minimum(tallies[donor] - 1, most - tallies[receiver]) // 2
    room = jnp.where((donor == order[0]) | (receiver == order[0]) | (tallies[receiver] == 0), 0, jnp.maximum(room, 0))
    moved = jax.random.randint(jax.random.fold_in(own, 4), (count // 2,), 0, 1 << 20) % (room + 1)
    tallies = tallies.at[donor].add(-moved).at[receiver].add(moved)
    items = jnp.searchsorted(jnp.cumsum(tallies), jnp.arange(rows * top), side="right").astype(jnp.int32)
    grid = items.reshape(top, rows).T
    grid = grid[jax.random.permutation(jax.random.fold_in(own, 1), rows)]
    turn = jax.random.randint(jax.random.fold_in(own, 2), (rows, 1), 0, top)
    return jnp.take_along_axis(grid, (jnp.arange(top)[None, :] + turn) % top, axis=1)


def load_shares(number_of, total, bound, slope, full):
    portions = [(1 << 20) // math.isqrt(grade ** slope) + 1 for grade in range(1, number_of + 1)]
    largest = bound if full else min(bound, max(-(-total // number_of), total * portions[0] // sum(portions)))
    least = 1 if total - largest >= number_of - 1 else 0
    counts, spare = [largest] + [least] * (number_of - 1), total - largest - least * (number_of - 1)
    while spare > 0:
        movable = [i for i in range(1, number_of) if counts[i] < largest] or [i for i in range(1, number_of) if counts[i] < bound]
        pool, remaining = sum([portions[i] for i in movable]), spare
        for i in movable:
            extra = min(bound - counts[i], max(1, remaining * portions[i] // pool), spare)
            counts[i] = counts[i] + extra
            spare = spare - extra
    return np.array(counts)


def bell_draw(key, shape, scale, limit, shards=(), held_as=jnp.bfloat16):
    result = jax.random.normal(key, shape, jnp.float32) * scale
    if len(shards) > 0:
        result = shard_levels(key, shape, shards, -0.22, 0.18) * result
    return jnp.clip(result, min=-limit, max=limit).astype(held_as)


def setup_inputs(seed: int = 0) -> dict:
    splits = jax.random.split(jax.random.key(seed), 12)
    fwd_sent = bell_draw(splits[0], (LAYERS, TOKENS, D), 1.0, 6.0, ((0, 8), (1, 64)))
    grad_sent = bell_draw(splits[1], (LAYERS, TOKENS, D), 1.0, 6.0, ((0, 8), (1, 64)))
    saved_scale = jnp.clip(jnp.exp(math.log(2.0) - 1.3862944 * jax.random.uniform(splits[2], (LAYERS, TOKENS), jnp.float32) ** shard_levels(splits[2], (LAYERS, TOKENS), ((0, 8), (1, 64)), -0.2, 0.2)), 0.5, 2.0)
    norm_gain = jnp.clip(1.0 + 0.18 * jax.random.normal(splits[3], (LAYERS, D), jnp.float32), 0.1, 1.9)
    w_in = bell_draw(splits[4], (LAYERS, N_EXPERT, D, 2 * H_DEV), D ** -0.5, 0.09375, ((0, 8), (1, 64)))
    w_down = bell_draw(splits[5], (LAYERS, N_EXPERT, H_DEV, D), EXP_HIDDEN ** -0.5, 0.1875, ((0, 8), (1, 64)))
    saved_pre = bell_draw(splits[6], (LAYERS, N_EXPERT, N_EXPERT * CAP, 2 * H_DEV), 1.0, 5.0, ((0, 8), (1, 64)))
    route_fwd_keys = jax.random.split(jax.random.fold_in(splits[7], 1), LAYERS * TOKENS // TOK_DEV)
    route_fwd_turns = jax.random.permutation(jax.random.fold_in(splits[7], 3), LAYERS * TOKENS // TOK_DEV)
    route_fwd = jax.vmap(lambda own, number: assign_block(jax.random.fold_in(splits[7], 2), own, number, TOK_DEV, EXPERTS, TOP, CAP, 0))(route_fwd_keys, route_fwd_turns).reshape((LAYERS, TOKENS, TOP))
    route_bwd_keys = jax.random.split(jax.random.fold_in(splits[8], 1), LAYERS * TOKENS // TOK_DEV)
    route_bwd_turns = jax.random.permutation(jax.random.fold_in(splits[8], 3), LAYERS * TOKENS // TOK_DEV)
    route_bwd = jax.vmap(lambda own, number: assign_block(jax.random.fold_in(splits[8], 2), own, number, TOK_DEV, EXPERTS, TOP, CAP, 0))(route_bwd_keys, route_bwd_turns).reshape((LAYERS, TOKENS, TOP))
    weight_fwd = jnp.clip(0.2 + 0.8 * jax.random.uniform(splits[9], (LAYERS, TOKENS), jnp.float32) ** shard_levels(splits[9], (LAYERS, TOKENS), ((0, 8), (1, 64)), -0.2, 0.2), 0.2, 1.0)
    weight_bwd = jnp.clip(0.2 + 0.8 * jax.random.uniform(splits[10], (LAYERS, TOKENS), jnp.float32) ** shard_levels(splits[10], (LAYERS, TOKENS), ((0, 8), (1, 64)), -0.2, 0.2), 0.2, 1.0)
    return dict(fwd_sent=fwd_sent, grad_sent=grad_sent, saved_scale=saved_scale, norm_gain=norm_gain, w_in=w_in, w_down=w_down, saved_pre=saved_pre, route_fwd=route_fwd, route_bwd=route_bwd, weight_fwd=weight_fwd, weight_bwd=weight_bwd)


EPSILON = 1e-06

def slot_positions(choices):
    expert_ids = jnp.arange(EXPERTS, dtype=jnp.int32)
    onehot = (choices[:, None] == expert_ids[None, :]).astype(jnp.int32)
    earlier = jnp.cumsum(onehot, axis=0) - onehot
    slot_rank = lax.optimization_barrier(jnp.sum(earlier * onehot, axis=1))
    return (choices * CAP + slot_rank).astype(jnp.int32)

def slot_table(positions):
    columns = jnp.arange(EXPERTS * CAP, dtype=jnp.int32)
    return (positions[:, None] == columns[None, :]).astype(jnp.bfloat16)

def normalize(values, gain_row):
    inverse = lax.rsqrt(lax.optimization_barrier(jnp.mean(values * values, axis=-1, keepdims=True)) + EPSILON)
    return (values * inverse * gain_row, inverse)

def expert_rows(tokens, choices):
    blocks = tokens.reshape(N_EXPERT, TOK_DEV, D).astype(jnp.float32)
    positions = jax.vmap(slot_positions)(choices.reshape(N_EXPERT, TOK_DEV).astype(jnp.int32))
    tables = jax.vmap(slot_table)(positions).astype(jnp.float32)
    packed = jnp.einsum('btp,btd->bpd', tables, blocks, precision=lax.Precision.HIGHEST).astype(jnp.bfloat16)
    per_expert = packed.reshape(N_EXPERT, EXPERTS, CAP, D).transpose(1, 0, 2, 3)
    return (per_expert.reshape(EXPERTS, N_EXPERT * CAP, D), positions)

def pick_rows(source_rows, positions):
    return jnp.take(source_rows, positions, axis=0)

def return_rows(summed, positions):
    by_source = summed.reshape(EXPERTS, N_EXPERT, CAP, D).transpose(1, 0, 2, 3)
    by_source = by_source.reshape(N_EXPERT, EXPERTS * CAP, D)
    picked = jax.vmap(pick_rows)(by_source, positions)
    return picked.reshape(N_EXPERT * TOK_DEV, D)

def forward_slice(row_block, weights_in, weights_down, saved):
    pre_act = jnp.dot(row_block, weights_in, preferred_element_type=jnp.float32)
    half_width = weights_in.shape[1] // 2
    hidden_act = (jax.nn.silu(pre_act[:, :half_width]) * pre_act[:, half_width:]).astype(jnp.bfloat16)
    return jnp.dot(hidden_act, weights_down, preferred_element_type=jnp.float32).astype(jnp.bfloat16)

def backward_slice(row_block, weights_in, weights_down, saved):
    contract_dims = (((1,), (1,)), ((), ()))
    grad_act = lax.dot_general(row_block, weights_down, contract_dims, preferred_element_type=jnp.float32)
    half_width = saved.shape[1] // 2
    pre_act = saved.astype(jnp.float32)
    gate_pre = pre_act[:, :half_width]
    up_pre = pre_act[:, half_width:]
    sigmoid_gate = jax.nn.sigmoid(gate_pre)
    grad_gate = grad_act * up_pre * sigmoid_gate * (1.0 + gate_pre * (1.0 - sigmoid_gate))
    grad_up = grad_act * gate_pre * sigmoid_gate
    grad_pre = jnp.concatenate([grad_gate, grad_up], axis=1).astype(jnp.bfloat16)
    return lax.dot_general(grad_pre, weights_in, contract_dims, preferred_element_type=jnp.float32).astype(jnp.bfloat16)

def expert_sum(per_expert, layer_in, layer_down, layer_saved, slice_fn):

    def one_expert(expert):
        row_block = per_expert[expert]

        def one_piece(piece_idx):
            device = expert * SPLIT + piece_idx
            return slice_fn(row_block, layer_in[device], layer_down[device], layer_saved[device])
        pieces = lax.map(one_piece, jnp.arange(SPLIT, dtype=jnp.int32))
        return lax.optimization_barrier(jnp.sum(pieces.astype(jnp.float32), axis=0))
    return lax.map(one_expert, jnp.arange(EXPERTS, dtype=jnp.int32))

def reference(fwd_sent, grad_sent, saved_scale, norm_gain, w_in, w_down, saved_pre, route_fwd, route_bwd, weight_fwd, weight_bwd):
    forward_list = []
    backward_list = []
    for section_index in range(LAYERS):
        arrive = fwd_sent[(section_index - 1) % LAYERS].astype(jnp.float32)
        normed, _ = normalize(arrive, norm_gain[section_index])
        per_expert, positions = expert_rows(normed.astype(jnp.bfloat16), route_fwd[section_index, :, 0])
        summed = expert_sum(per_expert, w_in[section_index], w_down[section_index], saved_pre[section_index], forward_slice)
        mixture = return_rows(summed, positions)
        forward_list.append((arrive + weight_fwd[section_index][:, None] * mixture).astype(jnp.bfloat16))
        grad_back = grad_sent[(section_index + 1) % LAYERS].astype(jnp.float32)
        scaled = (grad_back * weight_bwd[section_index][:, None]).astype(jnp.bfloat16)
        per_expert_bwd, positions_bwd = expert_rows(scaled, route_bwd[section_index, :, 0])
        summed_bwd = expert_sum(per_expert_bwd, w_in[section_index], w_down[section_index], saved_pre[section_index], backward_slice)
        grad_norm = return_rows(summed_bwd, positions_bwd)
        grad_start = saved_scale[section_index][:, None] * norm_gain[section_index] * grad_norm
        backward_list.append((grad_back + grad_start).astype(jnp.bfloat16))
    return (jnp.stack(forward_list), jnp.stack(backward_list))
```

```python
import jax
import jax.numpy as jnp
from jax import lax
from jax.experimental import pallas as pl
from jax.experimental.pallas import tpu as pltpu
from jax.sharding import PartitionSpec as P

EXPERTS = 8
CAP = 8
ROWS = 4
BLOCK = EXPERTS * CAP
EPSILON = 1e-06

FIRST = 2688
LAST = 896
DOWN = FIRST + LAST
NEXT = 2 * FIRST
TOTAL = NEXT + 256
WIDTH = 256
HIDDEN = 128
VMEM_LIMIT = 40 * 1024 * 1024


def shift_section(block, distance):
    size = lax.axis_size("section")
    return lax.ppermute(block, "section", [((i - distance) % size, i) for i in range(size)])


def shift_y(block, distance):
    size = lax.axis_size("expert")
    route = [(k, k - k % ROWS + (k + distance) % ROWS) for k in range(size)]
    return lax.ppermute(block, "expert", route)


def swap_z(block):
    size = lax.axis_size("expert")
    return lax.ppermute(block, "expert", [(k, k ^ ROWS) for k in range(size)])


def exchange_z(block):
    groups = [[2 * ROWS * g + r for g in range(EXPERTS)] for r in range(2 * ROWS)]
    return lax.all_to_all(
        block, "expert", split_axis=0, concat_axis=0, axis_index_groups=groups, tiled=True
    )


def exchange_halves(block):
    return jnp.concatenate([exchange_z(block[:, :CAP]), exchange_z(block[:, CAP:])], axis=1)


def as_column(row):
    size = row.shape[1]
    down = lax.broadcasted_iota(jnp.int32, (size, size), 0)
    across = lax.broadcasted_iota(jnp.int32, (size, size), 1)
    spread = jnp.where(down == across, jnp.broadcast_to(row, (size, size)), 0.0)
    return jnp.sum(spread, axis=1, keepdims=True)


def pack_kernel(route_fwd, route_bwd, arrive, grad_back, gain, weight, send, table):
    chosen = jnp.concatenate(
        [as_column(route[...].astype(jnp.float32)) for route in (route_fwd, route_bwd)], axis=0
    )
    shape = (2 * BLOCK, 2 * BLOCK)
    token = lax.broadcasted_iota(jnp.int32, shape, 0)
    column = lax.broadcasted_iota(jnp.int32, shape, 1)
    same = (column >> 4).astype(jnp.float32) == chosen
    same &= ((column >> 3) & 1) == (token >> 6)
    before = (column < token).astype(jnp.bfloat16)
    rank = mm(before, same.astype(jnp.bfloat16))
    onehot = (same & (rank == (column & 7).astype(jnp.float32))).astype(jnp.bfloat16)
    table[...] = onehot
    wide = arrive[...].astype(jnp.float32)
    inverse = lax.rsqrt(jnp.mean(wide * wide, axis=-1, keepdims=True) + EPSILON)
    normed = (wide * inverse * gain[...]).astype(jnp.bfloat16)
    scaled = (grad_back[...].astype(jnp.float32) * as_column(weight[...])).astype(jnp.bfloat16)
    tokens = jnp.concatenate([normed, scaled], axis=0)
    send[...] = lax.dot_general(
        onehot, tokens, (((0,), (0,)), ((), ())), preferred_element_type=jnp.float32
    ).astype(send.dtype)


def finish_kernel(table, back, arrive, grad_back, weight, scale, gain, forward_out, backward_out):
    got = mm(table[...], back[...])
    wide = arrive[...].astype(jnp.float32)
    forward_out[...] = (wide + as_column(weight[...]) * got[:BLOCK]).astype(forward_out.dtype)
    back_wide = grad_back[...].astype(jnp.float32)
    grad_start = as_column(scale[...]) * gain[...] * got[BLOCK:]
    backward_out[...] = (back_wide + grad_start).astype(backward_out.dtype)


def gather_kernel(in_own, down_own, saved_next, saved_previous, held, sems):
    count = down_own.shape[1] // WIDTH
    pieces = [
        (in_own, held.at[pl.ds(0, DOWN)]),
        (saved_next, held.at[pl.ds(NEXT, 128)]),
        (saved_previous, held.at[pl.ds(NEXT + 128, 128)]),
    ]
    for c in range(count):
        pieces.append(
            (
                down_own.at[:, pl.ds(c * WIDTH, WIDTH)],
                held.at[pl.ds(DOWN + c * HIDDEN, HIDDEN)],
            )
        )
    copies = [pltpu.make_async_copy(p[0], p[1], sems.at[i]) for i, p in enumerate(pieces)]
    for copy in copies:
        copy.start()
    for copy in copies:
        copy.wait()


def fetch(sources, buffers, sems):
    copies = [pltpu.make_async_copy(s, b, sems.at[i]) for i, (s, b) in enumerate(zip(sources, buffers))]
    for copy in copies:
        copy.start()
    return copies


def mm(a, b):
    return jnp.dot(a, b, preferred_element_type=jnp.float32)


def mt(a, b):
    return lax.dot_general(a, b, (((1,), (1,)), ((), ())), preferred_element_type=jnp.float32)


def activate(pre):
    gate, up = pre[:, :HIDDEN], pre[:, HIDDEN:]
    return (gate / (1.0 + jnp.exp(-gate)) * up).astype(jnp.bfloat16)


def slope(grad_act, saved):
    wide = saved.astype(jnp.float32)
    gate, up = wide[:, :HIDDEN], wide[:, HIDDEN:]
    sigmoid = 1.0 / (1.0 + jnp.exp(-gate))
    grad_gate = grad_act * up * sigmoid * (1.0 + gate * (1.0 - sigmoid))
    grad_up = grad_act * gate * sigmoid
    return jnp.concatenate([grad_gate, grad_up], axis=1).astype(jnp.bfloat16)


def down_blocks(held, start, count):
    return [held[start + c * HIDDEN : start + (c + 1) * HIDDEN] for c in range(count)]


def across_blocks(rows, held, start):
    count = rows.shape[1] // WIDTH
    total = 0.0
    for c, block in enumerate(down_blocks(held, start, count)):
        total = total + mt(rows[:, c * WIDTH : (c + 1) * WIDTH], block)
    return total


def near_kernel(rows_fwd, rows_bwd, saved_own, *refs):
    sources, part, grad_part, buffers, sems = refs[:4], refs[4], refs[5], refs[6:10], refs[10]
    copies = fetch(sources, buffers, sems)
    own_in, own_down, behind, ahead = buffers
    count = rows_fwd.shape[1] // WIDTH
    copies[0].wait()
    copies[1].wait()
    acts = [activate(mm(rows_fwd[...], own_in[...]))]
    grads = [slope(mt(rows_bwd[...], own_down[...]), saved_own[...])]
    for i, near, saved in ((2, behind, NEXT), (3, ahead, NEXT + 128)):
        copies[i].wait()
        acts.append(activate(mm(rows_fwd[...], near[:DOWN])))
        grads.append(slope(across_blocks(rows_bwd, near, DOWN), near[saved : saved + 128]))
    for c in range(count):
        columns = slice(c * WIDTH, (c + 1) * WIDTH)
        block = slice(DOWN + c * HIDDEN, DOWN + (c + 1) * HIDDEN)
        total = mm(acts[0], own_down[:, columns])
        part[:, columns] = total + mm(acts[1], behind[block]) + mm(acts[2], ahead[block])
    for c in range(count * WIDTH // LAST):
        columns = slice(c * LAST, (c + 1) * LAST)
        total = mt(grads[0], own_in[columns])
        grad_part[:, columns] = total + mt(grads[1], behind[columns]) + mt(grads[2], ahead[columns])


def forward_kernel(rows, part, *refs):
    sources, out, buffers, sems = refs[:2], refs[2], refs[3:5], refs[5]
    copies = fetch(sources, buffers, sems)
    far_a, far_b = buffers
    copies[0].wait()
    pre = mm(rows[:, :FIRST], far_a[...])
    copies[1].wait()
    act = activate(pre + mm(rows[:, FIRST:], far_b[:LAST]))
    count = rows.shape[1] // WIDTH
    for c, block in enumerate(down_blocks(far_b, LAST, count)):
        columns = slice(c * WIDTH, (c + 1) * WIDTH)
        out[:, columns] = (part[:, columns] + mm(act, block)).astype(out.dtype)


def backward_kernel(rows, part, saved, *refs):
    sources, out, buffers, sems = refs[:2], refs[2], refs[3:5], refs[5]
    copies = fetch(sources, buffers, sems)
    far_a, far_b = buffers
    copies[0].wait()
    copies[1].wait()
    grad = slope(across_blocks(rows, far_b, LAST), saved[...])
    for c in range(rows.shape[1] // LAST):
        columns = slice(c * LAST, (c + 1) * LAST)
        weights = far_a[columns] if c * LAST < FIRST else far_b[:LAST]
        out[:, columns] = (part[:, columns] + mt(grad, weights)).astype(out.dtype)


def call(kernel, outs, whole, held=(), flops=0, traffic=8_000_000):
    in_vmem, left = pl.BlockSpec(memory_space=pltpu.VMEM), pl.BlockSpec(memory_space=pl.ANY)
    scratch = [pltpu.VMEM(h.shape, h.dtype) for h in held]
    scratch += [pltpu.SemaphoreType.DMA((len(held),))] if held else []
    return pl.pallas_call(
        kernel,
        out_shape=[jax.ShapeDtypeStruct(shape, dtype) for shape, dtype in outs],
        in_specs=[in_vmem] * len(whole) + [left] * len(held),
        out_specs=[in_vmem] * len(outs),
        scratch_shapes=scratch,
        compiler_params=pltpu.CompilerParams(vmem_limit_bytes=VMEM_LIMIT),
        cost_estimate=pl.CostEstimate(flops=flops, bytes_accessed=traffic, transcendentals=0),
    )(*whole, *held)


def shards(
    fwd_sent,
    grad_sent,
    saved_scale,
    norm_gain,
    w_in,
    w_down,
    saved_pre,
    route_fwd,
    route_bwd,
    weight_fwd,
    weight_bwd,
):
    features = fwd_sent.shape[2]
    place = lax.axis_index("expert")
    y = place % ROWS
    parity = (place // ROWS) % 2
    in_own, down_own = w_in[0, 0], w_down[0, 0]

    by_source = saved_pre[0, 0].reshape(EXPERTS, 2, ROWS, CAP, WIDTH)

    def saved_for(distance):
        column = lax.dynamic_index_in_dim(by_source, (y + distance) % ROWS, 2, keepdims=False)
        mine = lax.dynamic_index_in_dim(column, parity, 1, keepdims=False)
        other = lax.dynamic_index_in_dim(column, 1 - parity, 1, keepdims=False)
        return jnp.concatenate([mine, other]).reshape(-1, WIDTH)

    left = pl.BlockSpec(memory_space=pl.ANY)
    held = pl.pallas_call(
        gather_kernel,
        out_shape=jax.ShapeDtypeStruct((TOTAL, WIDTH), in_own.dtype),
        in_specs=[left] * 4,
        out_specs=pl.BlockSpec(memory_space=pltpu.VMEM),
        scratch_shapes=[pltpu.SemaphoreType.DMA((3 + features // WIDTH,))],
        cost_estimate=pl.CostEstimate(flops=0, bytes_accessed=6_000_000, transcendentals=0),
    )(in_own, down_own, saved_for(1), saved_for(-1))
    behind, ahead = shift_y(held, 1), shift_y(held, -1)

    arrive = shift_section(fwd_sent[0], 1)
    grad_back = shift_section(grad_sent[0], -1)
    wide, narrow = (BLOCK, features), (2 * BLOCK, features)
    send, table = call(
        pack_kernel,
        [(narrow, jnp.bfloat16), ((2 * BLOCK, 2 * BLOCK), jnp.bfloat16)],
        (route_fwd.reshape(1, BLOCK), route_bwd.reshape(1, BLOCK), arrive, grad_back, norm_gain, weight_bwd),
        traffic=2_000_000,
    )
    own = lax.cond(
        route_fwd[0, 0, 0] >= 0,
        exchange_z,
        exchange_halves,
        send.reshape(EXPERTS, 2 * CAP, features),
    )
    behind, ahead, saved_across = lax.optimization_barrier((behind, ahead, saved_for(2)))
    saved_across = shift_y(saved_across, 2)
    partner = swap_z(own)
    far_a = shift_y(behind[:FIRST], 1)
    far_b = shift_y(ahead[FIRST:NEXT], -1)
    rows = jnp.stack([own, partner]).reshape(2 * EXPERTS, 2, CAP, features)
    rows_fwd = rows[:, 0].reshape(-1, features)
    rows_bwd = rows[:, 1].reshape(-1, features)

    part, grad_part = call(
        near_kernel,
        [(narrow, jnp.float32)] * 2,
        (rows_fwd, rows_bwd, saved_for(0)),
        (in_own, down_own, behind, ahead),
        flops=2_100_000_000,
    )
    far = (far_a, far_b)
    (part,) = call(forward_kernel, [(narrow, jnp.bfloat16)], (rows_fwd, part), far, 350_000_000)
    received_fwd = swap_z(part[BLOCK:])
    (grad_part,) = call(backward_kernel, [(narrow, jnp.bfloat16)], (rows_bwd, grad_part, saved_across), far, 350_000_000)
    received_bwd = swap_z(grad_part[BLOCK:])

    def add(product, received):
        total = product[:BLOCK].astype(jnp.float32) + received.astype(jnp.float32)
        return total.astype(jnp.bfloat16).reshape(EXPERTS, CAP, features)

    sums = [add(part, received_fwd), add(grad_part, received_bwd)]
    back = exchange_z(jnp.concatenate(sums, axis=1)).reshape(narrow)
    forward_out, backward_out = call(
        finish_kernel,
        [(wide, jnp.bfloat16)] * 2,
        (table, back, arrive, grad_back, weight_fwd, saved_scale, norm_gain),
    )
    return (forward_out[None], backward_out[None])


def solution(mesh):
    in_specs = (
        P("section", "expert", None),
        P("section", "expert", None),
        P("section", "expert"),
        P("section", None),
        P("section", "expert", None, None),
        P("section", "expert", None, None),
        P("section", "expert", None, None),
        P("section", "expert", None),
        P("section", "expert", None),
        P("section", "expert"),
        P("section", "expert"),
    )
    out_specs = (P("section", "expert", None), P("section", "expert", None))
    return jax.shard_map(shards, mesh=mesh, in_specs=in_specs, out_specs=out_specs, check_vma=False)
```

```python
import jax
import jax.numpy as jnp
from jax import lax
from jax.experimental import pallas as pl
from jax.experimental.pallas import tpu as pltpu
from jax.sharding import PartitionSpec as P

EXPERTS = 8
CAP = 8
ROWS = 4
BLOCK = EXPERTS * CAP
EPSILON = 1e-06

FIRST = 1792
LAST = 1792
PART = 8
ACROSS = 1792
NEXT = ACROSS + 128
TOTAL = NEXT + 256
CHUNKS = ((0, 896), (896, 896), (FIRST, 896), (FIRST + 896, 896))
WIDTH = 256
HIDDEN = 128
VMEM_LIMIT = 40 * 1024 * 1024


def shift_section(block, distance):
    size = lax.axis_size("section")
    return lax.ppermute(block, "section", [((i - distance) % size, i) for i in range(size)])


def shift_y(block, distance):
    size = lax.axis_size("expert")
    route = [(k, k - k % ROWS + (k + distance) % ROWS) for k in range(size)]
    return lax.ppermute(block, "expert", route)


def swap_z(block):
    size = lax.axis_size("expert")
    return lax.ppermute(block, "expert", [(k, k ^ ROWS) for k in range(size)])


def exchange_z(block):
    groups = [[2 * ROWS * g + r for g in range(EXPERTS)] for r in range(2 * ROWS)]
    return lax.all_to_all(
        block, "expert", split_axis=0, concat_axis=0, axis_index_groups=groups, tiled=True
    )


def as_column(row):
    size = row.shape[1]
    down = lax.broadcasted_iota(jnp.int32, (size, size), 0)
    across = lax.broadcasted_iota(jnp.int32, (size, size), 1)
    spread = jnp.where(down == across, jnp.broadcast_to(row, (size, size)), 0.0)
    return jnp.sum(spread, axis=1, keepdims=True)


def pack_kernel(values, arrive, grad_back, send, table):
    features = arrive.shape[1]
    chosen = as_column(values[:, features : features + 128])
    weights = as_column(values[:, features + 128 : features + 256])
    shape = (2 * BLOCK, 2 * BLOCK)
    token = lax.broadcasted_iota(jnp.int32, shape, 0)
    column = lax.broadcasted_iota(jnp.int32, shape, 1)
    same = (column >> 4).astype(jnp.float32) == chosen
    same &= ((column >> 3) & 1) == (token >> 6)
    before = (column < token).astype(jnp.bfloat16)
    rank = mm(before, same.astype(jnp.bfloat16))
    onehot = (same & (rank == (column & 7).astype(jnp.float32))).astype(jnp.bfloat16)
    table[...] = onehot
    wide = arrive[...].astype(jnp.float32)
    inverse = lax.rsqrt(jnp.mean(wide * wide, axis=-1, keepdims=True) + EPSILON)
    normed = (wide * inverse * values[:, :features]).astype(jnp.bfloat16)
    scaled = (grad_back[...].astype(jnp.float32) * weights[BLOCK:]).astype(jnp.bfloat16)
    tokens = jnp.concatenate([normed, scaled], axis=0)
    send[...] = lax.dot_general(
        onehot, tokens, (((0,), (0,)), ((), ())), preferred_element_type=jnp.float32
    ).astype(send.dtype)


def finish_kernel(values, table, back, arrive, grad_back, forward_out, backward_out):
    features = arrive.shape[1]
    weights = as_column(values[:, features + 128 : features + 256])
    scales = as_column(values[:, features + 256 :])
    got = mm(table[...], back[...])
    wide = arrive[...].astype(jnp.float32)
    forward_out[...] = (wide + weights[:BLOCK] * got[:BLOCK]).astype(forward_out.dtype)
    back_wide = grad_back[...].astype(jnp.float32)
    grad_start = scales[BLOCK:] * values[:, :features] * got[BLOCK:]
    backward_out[...] = (back_wide + grad_start).astype(backward_out.dtype)


def gather_kernel(down_own, saved_across, saved_next, saved_previous, held, sems):
    pieces = [
        (saved_across, held.at[pl.ds(ACROSS, 128)]),
        (saved_next, held.at[pl.ds(NEXT, 128)]),
        (saved_previous, held.at[pl.ds(NEXT + 128, 128)]),
    ]
    for c in range(down_own.shape[1] // WIDTH):
        pieces.append(
            (
                down_own.at[:, pl.ds(c * WIDTH, WIDTH)],
                held.at[pl.ds(c * HIDDEN, HIDDEN)],
            )
        )
    copies = [pltpu.make_async_copy(p[0], p[1], sems.at[i]) for i, p in enumerate(pieces)]
    for copy in copies:
        copy.start()
    for copy in copies:
        copy.wait()


def fetch(sources, buffers, sems):
    copies = [pltpu.make_async_copy(s, b, sems.at[i]) for i, (s, b) in enumerate(zip(sources, buffers))]
    for copy in copies:
        copy.start()
    return copies


def mm(a, b):
    return jnp.dot(a, b, preferred_element_type=jnp.float32)


def mt(a, b):
    return lax.dot_general(a, b, (((1,), (1,)), ((), ())), preferred_element_type=jnp.float32)


def activate(pre):
    gate, up = pre[:, :HIDDEN], pre[:, HIDDEN:]
    return (gate / (1.0 + jnp.exp(-gate)) * up).astype(jnp.bfloat16)


def factors(saved):
    wide = saved.astype(jnp.float32)
    gate, up = wide[:, :HIDDEN], wide[:, HIDDEN:]
    sigmoid = 1.0 / (1.0 + jnp.exp(-gate))
    return up * sigmoid * (1.0 + gate * (1.0 - sigmoid)), gate * sigmoid


def slope(grad_act, gate_factor, up_factor):
    return jnp.concatenate([grad_act * gate_factor, grad_act * up_factor], axis=1).astype(
        jnp.bfloat16
    )


def factor_kernel(own, behind, ahead, out):
    for i, saved in enumerate((own, behind, ahead)):
        rows = slice(i * 128, (i + 1) * 128)
        out[rows, :HIDDEN], out[rows, HIDDEN:] = factors(saved[...])


def down_blocks(held, start, count):
    return [held[start + c * HIDDEN : start + (c + 1) * HIDDEN] for c in range(count)]


def across_blocks(rows, held, start):
    count = rows.shape[1] // WIDTH
    total = 0.0
    for c, block in enumerate(down_blocks(held, start, count)):
        total = total + mt(rows[:, c * WIDTH : (c + 1) * WIDTH], block)
    return total


def near_kernel(rows_fwd, rows_bwd, factor, *refs):
    sources, part, grad_part, buffers, sems = refs[:6], refs[6], refs[7], refs[8:14], refs[14]
    copies = fetch(sources, buffers, sems)
    own_in, own_down, behind_in, behind, ahead_in, ahead = buffers
    count = rows_fwd.shape[1] // WIDTH

    def scaled(i, grad_act):
        rows = slice(i * 128, (i + 1) * 128)
        return slope(grad_act, factor[rows, :HIDDEN], factor[rows, HIDDEN:])

    copies[0].wait()
    copies[1].wait()
    acts = [activate(mm(rows_fwd[...], own_in[...]))]
    grads = [scaled(0, mt(rows_bwd[...], own_down[...]))]
    for i, near_in, near in ((1, behind_in, behind), (2, ahead_in, ahead)):
        copies[2 * i].wait()
        copies[2 * i + 1].wait()
        acts.append(activate(mm(rows_fwd[...], near_in[...])))
        grads.append(scaled(i, across_blocks(rows_bwd, near, 0)))
    for c in range(count):
        columns = slice(c * WIDTH, (c + 1) * WIDTH)
        block = slice(c * HIDDEN, (c + 1) * HIDDEN)
        total = mm(acts[0], own_down[:, columns])
        part[:, columns] = total + mm(acts[1], behind[block]) + mm(acts[2], ahead[block])
    for start, size in CHUNKS:
        columns = slice(start, start + size)
        total = mt(grads[0], own_in[columns])
        total += mt(grads[1], behind_in[columns]) + mt(grads[2], ahead_in[columns])
        grad_part[:, columns] = total


def forward_kernel(rows, part, *refs):
    sources, out, buffers, sems = refs[:4], refs[4], refs[5:9], refs[9]
    copies = fetch(sources, buffers, sems)
    first, last, down_first, down_last = buffers
    copies[0].wait()
    pre = mm(rows[:, :FIRST], first[...])
    copies[1].wait()
    act = activate(pre + mm(rows[:, FIRST:], last[...]))
    copies[2].wait()
    copies[3].wait()
    count = rows.shape[1] // WIDTH
    blocks = down_blocks(down_first, 0, PART) + down_blocks(down_last, 0, count - PART)
    for c, block in enumerate(blocks):
        columns = slice(c * WIDTH, (c + 1) * WIDTH)
        out[:, columns] = (part[:, columns] + mm(act, block)).astype(out.dtype)


def backward_kernel(rows, part, *refs):
    sources, out, buffers, sems = refs[:4], refs[4], refs[5:9], refs[9]
    copies = fetch(sources, buffers, sems)
    first, last, down_first, down_last = buffers
    copies[2].wait()
    copies[3].wait()
    middle = PART * WIDTH
    grad_act = across_blocks(rows[:, :middle], down_first, 0)
    grad_act += across_blocks(rows[:, middle:], down_last, 0)
    grad = slope(grad_act, *factors(down_last[ACROSS - PART * HIDDEN :]))
    copies[0].wait()
    copies[1].wait()
    for start, size in CHUNKS:
        columns = slice(start, start + size)
        weights = first[columns] if start < FIRST else last[start - FIRST : start - FIRST + size]
        out[:, columns] = (part[:, columns] + mt(grad, weights)).astype(out.dtype)


def halves_kernel(behind, ahead, first, last, sems):
    one = pltpu.make_async_copy(behind.at[pl.ds(0, FIRST)], first, sems.at[0])
    two = pltpu.make_async_copy(ahead.at[pl.ds(FIRST, LAST)], last, sems.at[1])
    one.start()
    two.start()
    one.wait()
    two.wait()


def call(kernel, outs, whole, held=(), flops=0, traffic=8_000_000):
    in_vmem, left = pl.BlockSpec(memory_space=pltpu.VMEM), pl.BlockSpec(memory_space=pl.ANY)
    scratch = [pltpu.VMEM(h.shape, h.dtype) for h in held]
    scratch += [pltpu.SemaphoreType.DMA((len(held),))] if held else []
    return pl.pallas_call(
        kernel,
        out_shape=[jax.ShapeDtypeStruct(shape, dtype) for shape, dtype in outs],
        in_specs=[in_vmem] * len(whole) + [left] * len(held),
        out_specs=[in_vmem] * len(outs),
        scratch_shapes=scratch,
        compiler_params=pltpu.CompilerParams(vmem_limit_bytes=VMEM_LIMIT),
        cost_estimate=pl.CostEstimate(flops=flops, bytes_accessed=traffic, transcendentals=0),
    )(*whole, *held)


def shards(
    fwd_sent,
    grad_sent,
    saved_scale,
    norm_gain,
    w_in,
    w_down,
    saved_pre,
    route_fwd,
    route_bwd,
    weight_fwd,
    weight_bwd,
):
    features = fwd_sent.shape[2]
    place = lax.axis_index("expert")
    y = place % ROWS
    parity = (place // ROWS) % 2
    in_own, down_own = w_in[0, 0], w_down[0, 0]

    by_source = saved_pre[0, 0].reshape(EXPERTS, 2, ROWS, CAP, WIDTH)

    def saved_for(distance):
        column = lax.dynamic_index_in_dim(by_source, (y + distance) % ROWS, 2, keepdims=False)
        mine = lax.dynamic_index_in_dim(column, parity, 1, keepdims=False)
        other = lax.dynamic_index_in_dim(column, 1 - parity, 1, keepdims=False)
        return jnp.concatenate([mine, other]).reshape(-1, WIDTH)

    left = pl.BlockSpec(memory_space=pl.ANY)
    held = pl.pallas_call(
        gather_kernel,
        out_shape=jax.ShapeDtypeStruct((TOTAL, WIDTH), in_own.dtype),
        in_specs=[left] * 4,
        out_specs=pl.BlockSpec(memory_space=pltpu.VMEM),
        scratch_shapes=[pltpu.SemaphoreType.DMA((3 + features // WIDTH,))],
        cost_estimate=pl.CostEstimate(flops=0, bytes_accessed=2_000_000, transcendentals=0),
    )(down_own, saved_for(2), saved_for(1), saved_for(-1))
    behind_in, ahead_in = shift_y(in_own, 1), shift_y(in_own, -1)
    behind, ahead = shift_y(held, 1), shift_y(held, -1)

    routes = [route.reshape(1, BLOCK).astype(jnp.float32) for route in (route_fwd, route_bwd)]
    values = jnp.concatenate(
        [norm_gain, *routes, weight_fwd, weight_bwd, saved_scale, saved_scale], axis=1
    )
    arrive = shift_section(fwd_sent[0], 1)
    grad_back = shift_section(grad_sent[0], -1)
    wide, narrow = (BLOCK, features), (2 * BLOCK, features)
    send, table = call(
        pack_kernel,
        [(narrow, jnp.bfloat16), ((2 * BLOCK, 2 * BLOCK), jnp.bfloat16)],
        (values, arrive, grad_back),
        flops=20_000_000_000,
    )
    own = exchange_z(send.reshape(EXPERTS, 2 * CAP, features))
    halves = pl.pallas_call(
        halves_kernel,
        out_shape=[jax.ShapeDtypeStruct((n, WIDTH), in_own.dtype) for n in (FIRST, LAST)],
        in_specs=[left] * 2,
        out_specs=[pl.BlockSpec(memory_space=pltpu.VMEM)] * 2,
        scratch_shapes=[pltpu.SemaphoreType.DMA((2,))],
        cost_estimate=pl.CostEstimate(flops=20_000_000_000, bytes_accessed=4_000_000, transcendentals=0),
    )(behind_in, ahead_in)
    far_in = (shift_y(halves[0], 1), shift_y(halves[1], -1))
    partner = swap_z(own)
    far_in, partner, saved_behind = lax.optimization_barrier(
        (far_in, partner, behind[NEXT : NEXT + 128])
    )
    (factor,) = call(
        factor_kernel,
        [((384, WIDTH), jnp.float32)],
        (saved_for(0), saved_behind, ahead[NEXT + 128 :]),
        flops=1_000_000_000,
    )
    far_down = (
        shift_y(behind[: PART * HIDDEN], 1),
        shift_y(ahead[PART * HIDDEN : NEXT], -1),
    )
    far = (*far_in, *far_down)
    rows = jnp.stack([own, partner]).reshape(2 * EXPERTS, 2, CAP, features)
    rows_fwd = rows[:, 0].reshape(-1, features)
    rows_bwd = rows[:, 1].reshape(-1, features)

    part, grad_part = call(
        near_kernel,
        [(narrow, jnp.float32)] * 2,
        (rows_fwd, rows_bwd, factor),
        (in_own, down_own, behind_in, behind, ahead_in, ahead),
        flops=2_000_000_000,
        traffic=0,
    )
    (part,) = call(forward_kernel, [(narrow, jnp.bfloat16)], (rows_fwd, part), far, 350_000_000)
    received_fwd = swap_z(part[BLOCK:])
    (grad_part,) = call(backward_kernel, [(narrow, jnp.bfloat16)], (rows_bwd, grad_part), far, 350_000_000)
    received_bwd = swap_z(grad_part[BLOCK:])

    def add(product, received):
        total = product[:BLOCK].astype(jnp.float32) + received.astype(jnp.float32)
        return total.astype(jnp.bfloat16).reshape(EXPERTS, CAP, features)

    sums = [add(part, received_fwd), add(grad_part, received_bwd)]
    back = exchange_z(jnp.concatenate(sums, axis=1)).reshape(narrow)
    forward_out, backward_out = call(
        finish_kernel,
        [(wide, jnp.bfloat16)] * 2,
        (values, table, back, arrive, grad_back),
    )
    return (forward_out[None], backward_out[None])


def solution(mesh):
    in_specs = (
        P("section", "expert", None),
        P("section", "expert", None),
        P("section", "expert"),
        P("section", None),
        P("section", "expert", None, None),
        P("section", "expert", None, None),
        P("section", "expert", None, None),
        P("section", "expert", None),
        P("section", "expert", None),
        P("section", "expert"),
        P("section", "expert"),
    )
    out_specs = (P("section", "expert", None), P("section", "expert", None))
    return jax.shard_map(shards, mesh=mesh, in_specs=in_specs, out_specs=out_specs, check_vma=False)
```

```python
import jax
import jax.numpy as jnp
from jax import lax
from jax.experimental import pallas as pl
from jax.experimental.pallas import tpu as pltpu
from jax.sharding import PartitionSpec as P

EXPERTS = 8
CAP = 8
ROWS = 4
BLOCK = EXPERTS * CAP
EPSILON = 1e-06

FIRST = 1792
LAST = 1792
PART = 8
ACROSS = 1792
NEXT = ACROSS + 128
TOTAL = NEXT + 128
CHUNKS = ((0, 896), (896, 896), (FIRST, 896), (FIRST + 896, 896))
WIDTH = 256
HIDDEN = 128
VMEM_LIMIT = 40 * 1024 * 1024


def shift_section(block, distance):
    size = lax.axis_size("section")
    return lax.ppermute(block, "section", [((i - distance) % size, i) for i in range(size)])


def shift_y(block, distance):
    size = lax.axis_size("expert")
    route = [(k, k - k % ROWS + (k + distance) % ROWS) for k in range(size)]
    return lax.ppermute(block, "expert", route)


def swap_z(block):
    size = lax.axis_size("expert")
    return lax.ppermute(block, "expert", [(k, k ^ ROWS) for k in range(size)])


def exchange_z(block):
    groups = [[2 * ROWS * g + r for g in range(EXPERTS)] for r in range(2 * ROWS)]
    return lax.all_to_all(
        block, "expert", split_axis=0, concat_axis=0, axis_index_groups=groups, tiled=True
    )


def as_column(row):
    size = row.shape[1]
    down = lax.broadcasted_iota(jnp.int32, (size, size), 0)
    across = lax.broadcasted_iota(jnp.int32, (size, size), 1)
    spread = jnp.where(down == across, jnp.broadcast_to(row, (size, size)), 0.0)
    return jnp.sum(spread, axis=1, keepdims=True)


def pack_kernel(values, arrive, grad_back, send, table):
    features = arrive.shape[1]
    chosen = as_column(values[:, features : features + 128])
    weights = as_column(values[:, features + 128 : features + 256])
    shape = (2 * BLOCK, 2 * BLOCK)
    token = lax.broadcasted_iota(jnp.int32, shape, 0)
    column = lax.broadcasted_iota(jnp.int32, shape, 1)
    same = (column >> 4).astype(jnp.float32) == chosen
    same &= ((column >> 3) & 1) == (token >> 6)
    before = (column < token).astype(jnp.bfloat16)
    rank = mm(before, same.astype(jnp.bfloat16))
    onehot = (same & (rank == (column & 7).astype(jnp.float32))).astype(jnp.bfloat16)
    table[...] = onehot
    wide = arrive[...].astype(jnp.float32)
    inverse = lax.rsqrt(jnp.mean(wide * wide, axis=-1, keepdims=True) + EPSILON)
    normed = (wide * inverse * values[:, :features]).astype(jnp.bfloat16)
    scaled = (grad_back[...].astype(jnp.float32) * weights[BLOCK:]).astype(jnp.bfloat16)
    tokens = jnp.concatenate([normed, scaled], axis=0)
    send[...] = lax.dot_general(
        onehot, tokens, (((0,), (0,)), ((), ())), preferred_element_type=jnp.float32
    ).astype(send.dtype)


def finish_kernel(values, table, back, arrive, grad_back, forward_out, backward_out):
    features = arrive.shape[1]
    weights = as_column(values[:, features + 128 : features + 256])
    scales = as_column(values[:, features + 256 :])
    got = mm(table[...], back[...])
    wide = arrive[...].astype(jnp.float32)
    forward_out[...] = (wide + weights[:BLOCK] * got[:BLOCK]).astype(forward_out.dtype)
    back_wide = grad_back[...].astype(jnp.float32)
    grad_start = scales[BLOCK:] * values[:, :features] * got[BLOCK:]
    backward_out[...] = (back_wide + grad_start).astype(backward_out.dtype)


def gather_kernel(down_own, saved_across, saved_next, saved_previous, held_next, held_previous, sems):
    pieces = []
    for held, saved in ((held_next, saved_next), (held_previous, saved_previous)):
        pieces.append((saved_across, held.at[pl.ds(ACROSS, 128)]))
        pieces.append((saved, held.at[pl.ds(NEXT, 128)]))
        for c in range(down_own.shape[1] // WIDTH):
            block = down_own.at[:, pl.ds(c * WIDTH, WIDTH)]
            pieces.append((block, held.at[pl.ds(c * HIDDEN, HIDDEN)]))
    copies = [pltpu.make_async_copy(p[0], p[1], sems.at[i]) for i, p in enumerate(pieces)]
    for copy in copies:
        copy.start()
    for copy in copies:
        copy.wait()


def fetch(sources, buffers, sems):
    copies = [pltpu.make_async_copy(s, b, sems.at[i]) for i, (s, b) in enumerate(zip(sources, buffers))]
    for copy in copies:
        copy.start()
    return copies


def mm(a, b):
    return jnp.dot(a, b, preferred_element_type=jnp.float32)


def mt(a, b):
    return lax.dot_general(a, b, (((1,), (1,)), ((), ())), preferred_element_type=jnp.float32)


def activate(pre):
    gate, up = pre[:, :HIDDEN], pre[:, HIDDEN:]
    return (gate / (1.0 + jnp.exp(-gate)) * up).astype(jnp.bfloat16)


def factors(saved):
    wide = saved.astype(jnp.float32)
    gate, up = wide[:, :HIDDEN], wide[:, HIDDEN:]
    sigmoid = 1.0 / (1.0 + jnp.exp(-gate))
    return up * sigmoid * (1.0 + gate * (1.0 - sigmoid)), gate * sigmoid


def slope(grad_act, gate_factor, up_factor):
    return jnp.concatenate([grad_act * gate_factor, grad_act * up_factor], axis=1).astype(
        jnp.bfloat16
    )


def factor_kernel(own, behind, ahead, out):
    for i, saved in enumerate((own, behind, ahead)):
        rows = slice(i * 128, (i + 1) * 128)
        out[rows, :HIDDEN], out[rows, HIDDEN:] = factors(saved[...])


def down_blocks(held, start, count):
    return [held[start + c * HIDDEN : start + (c + 1) * HIDDEN] for c in range(count)]


def across_blocks(rows, held, start):
    count = rows.shape[1] // WIDTH
    total = 0.0
    for c, block in enumerate(down_blocks(held, start, count)):
        total = total + mt(rows[:, c * WIDTH : (c + 1) * WIDTH], block)
    return total


def near_kernel(rows_fwd, rows_bwd, factor, *refs):
    sources, part, grad_part, buffers, sems = refs[:6], refs[6], refs[7], refs[8:14], refs[14]
    copies = fetch(sources, buffers, sems)
    own_in, own_down, behind_in, behind, ahead_in, ahead = buffers
    count = rows_fwd.shape[1] // WIDTH

    def scaled(i, grad_act):
        rows = slice(i * 128, (i + 1) * 128)
        return slope(grad_act, factor[rows, :HIDDEN], factor[rows, HIDDEN:])

    copies[0].wait()
    copies[1].wait()
    acts = [activate(mm(rows_fwd[...], own_in[...]))]
    grads = [scaled(0, mt(rows_bwd[...], own_down[...]))]
    for i, near_in, near in ((1, behind_in, behind), (2, ahead_in, ahead)):
        copies[2 * i].wait()
        copies[2 * i + 1].wait()
        acts.append(activate(mm(rows_fwd[...], near_in[...])))
        grads.append(scaled(i, across_blocks(rows_bwd, near, 0)))
    for c in range(count):
        columns = slice(c * WIDTH, (c + 1) * WIDTH)
        block = slice(c * HIDDEN, (c + 1) * HIDDEN)
        total = mm(acts[0], own_down[:, columns])
        part[:, columns] = total + mm(acts[1], behind[block]) + mm(acts[2], ahead[block])
    for start, size in CHUNKS:
        columns = slice(start, start + size)
        total = mt(grads[0], own_in[columns])
        total += mt(grads[1], behind_in[columns]) + mt(grads[2], ahead_in[columns])
        grad_part[:, columns] = total


def forward_kernel(rows, part, *refs):
    first, last, down_first, down_last, out = refs
    pre = mm(rows[:, :FIRST], first[...])
    act = activate(pre + mm(rows[:, FIRST:], last[...]))
    count = rows.shape[1] // WIDTH
    blocks = down_blocks(down_first, 0, PART) + down_blocks(down_last, 0, count - PART)
    for c, block in enumerate(blocks):
        columns = slice(c * WIDTH, (c + 1) * WIDTH)
        out[:, columns] = (part[:, columns] + mm(act, block)).astype(out.dtype)


def backward_kernel(rows, part, *refs):
    first, last, down_first, down_last, out = refs
    middle = PART * WIDTH
    grad_act = across_blocks(rows[:, :middle], down_first, 0)
    grad_act += across_blocks(rows[:, middle:], down_last, 0)
    grad = slope(grad_act, *factors(down_last[ACROSS - PART * HIDDEN :]))
    for start, size in CHUNKS:
        columns = slice(start, start + size)
        weights = first[columns] if start < FIRST else last[start - FIRST : start - FIRST + size]
        out[:, columns] = (part[:, columns] + mt(grad, weights)).astype(out.dtype)


def halves_kernel(behind, ahead, first, last, sems):
    one = pltpu.make_async_copy(behind.at[pl.ds(0, FIRST)], first, sems.at[0])
    two = pltpu.make_async_copy(ahead.at[pl.ds(FIRST, LAST)], last, sems.at[1])
    one.start()
    two.start()
    one.wait()
    two.wait()


def call(kernel, outs, whole, held=(), flops=0, traffic=8_000_000):
    in_vmem, left = pl.BlockSpec(memory_space=pltpu.VMEM), pl.BlockSpec(memory_space=pl.ANY)
    scratch = [pltpu.VMEM(h.shape, h.dtype) for h in held]
    scratch += [pltpu.SemaphoreType.DMA((len(held),))] if held else []
    return pl.pallas_call(
        kernel,
        out_shape=[jax.ShapeDtypeStruct(shape, dtype) for shape, dtype in outs],
        in_specs=[in_vmem] * len(whole) + [left] * len(held),
        out_specs=[in_vmem] * len(outs),
        scratch_shapes=scratch,
        compiler_params=pltpu.CompilerParams(vmem_limit_bytes=VMEM_LIMIT),
        cost_estimate=pl.CostEstimate(flops=flops, bytes_accessed=traffic, transcendentals=0),
    )(*whole, *held)


def shards(
    fwd_sent,
    grad_sent,
    saved_scale,
    norm_gain,
    w_in,
    w_down,
    saved_pre,
    route_fwd,
    route_bwd,
    weight_fwd,
    weight_bwd,
):
    features = fwd_sent.shape[2]
    place = lax.axis_index("expert")
    y = place % ROWS
    parity = (place // ROWS) % 2
    in_own, down_own = w_in[0, 0], w_down[0, 0]

    by_source = saved_pre[0, 0].reshape(EXPERTS, 2, ROWS, CAP, WIDTH)

    def saved_for(distance):
        column = lax.dynamic_index_in_dim(by_source, (y + distance) % ROWS, 2, keepdims=False)
        mine = lax.dynamic_index_in_dim(column, parity, 1, keepdims=False)
        other = lax.dynamic_index_in_dim(column, 1 - parity, 1, keepdims=False)
        return jnp.concatenate([mine, other]).reshape(-1, WIDTH)

    left = pl.BlockSpec(memory_space=pl.ANY)
    held_next, held_previous = pl.pallas_call(
        gather_kernel,
        out_shape=[jax.ShapeDtypeStruct((TOTAL, WIDTH), in_own.dtype)] * 2,
        in_specs=[left] * 4,
        out_specs=[pl.BlockSpec(memory_space=pltpu.VMEM)] * 2,
        scratch_shapes=[pltpu.SemaphoreType.DMA((4 + 2 * (features // WIDTH),))],
        cost_estimate=pl.CostEstimate(flops=0, bytes_accessed=2_000_000, transcendentals=0),
    )(down_own, saved_for(2), saved_for(1), saved_for(-1))
    behind_in, ahead_in = shift_y(in_own, 1), shift_y(in_own, -1)
    behind, ahead = shift_y(held_next, 1), shift_y(held_previous, -1)

    routes = [route.reshape(1, BLOCK).astype(jnp.float32) for route in (route_fwd, route_bwd)]
    values = jnp.concatenate(
        [norm_gain, *routes, weight_fwd, weight_bwd, saved_scale, saved_scale], axis=1
    )
    arrive = shift_section(fwd_sent[0], 1)
    grad_back = shift_section(grad_sent[0], -1)
    wide, narrow = (BLOCK, features), (2 * BLOCK, features)
    send, table = call(
        pack_kernel,
        [(narrow, jnp.bfloat16), ((2 * BLOCK, 2 * BLOCK), jnp.bfloat16)],
        (values, arrive, grad_back),
        flops=20_000_000_000,
    )
    own = exchange_z(send.reshape(EXPERTS, 2 * CAP, features))
    halves = pl.pallas_call(
        halves_kernel,
        out_shape=[jax.ShapeDtypeStruct((n, WIDTH), in_own.dtype) for n in (FIRST, LAST)],
        in_specs=[left] * 2,
        out_specs=[pl.BlockSpec(memory_space=pltpu.VMEM)] * 2,
        scratch_shapes=[pltpu.SemaphoreType.DMA((2,))],
        cost_estimate=pl.CostEstimate(flops=20_000_000_000, bytes_accessed=4_000_000, transcendentals=0),
    )(behind_in, ahead_in)
    far_in = (shift_y(halves[0], 1), shift_y(halves[1], -1))
    partner = swap_z(own)
    far_in, partner, saved_behind = lax.optimization_barrier(
        (far_in, partner, behind[NEXT:])
    )
    (factor,) = call(
        factor_kernel,
        [((384, WIDTH), jnp.float32)],
        (saved_for(0), saved_behind, ahead[NEXT:]),
        flops=1_000_000_000,
    )
    far_down = (
        shift_y(behind[: PART * HIDDEN], 1),
        shift_y(ahead[PART * HIDDEN : NEXT], -1),
    )
    far = (*far_in, *far_down)
    rows = jnp.stack([own, partner]).reshape(2 * EXPERTS, 2, CAP, features)
    rows_fwd = rows[:, 0].reshape(-1, features)
    rows_bwd = rows[:, 1].reshape(-1, features)

    part, grad_part = call(
        near_kernel,
        [(narrow, jnp.float32)] * 2,
        (rows_fwd, rows_bwd, factor),
        (in_own, down_own, behind_in, behind, ahead_in, ahead),
        flops=2_000_000_000,
        traffic=0,
    )
    (part,) = call(forward_kernel, [(narrow, jnp.bfloat16)], (rows_fwd, part, *far), flops=350_000_000)
    received_fwd = swap_z(part[BLOCK:])
    (grad_part,) = call(backward_kernel, [(narrow, jnp.bfloat16)], (rows_bwd, grad_part, *far), flops=350_000_000)
    received_bwd = swap_z(grad_part[BLOCK:])

    def add(product, received):
        total = product[:BLOCK].astype(jnp.float32) + received.astype(jnp.float32)
        return total.astype(jnp.bfloat16).reshape(EXPERTS, CAP, features)

    sums = [add(part, received_fwd), add(grad_part, received_bwd)]
    back = exchange_z(jnp.concatenate(sums, axis=1)).reshape(narrow)
    forward_out, backward_out = call(
        finish_kernel,
        [(wide, jnp.bfloat16)] * 2,
        (values, table, back, arrive, grad_back),
    )
    return (forward_out[None], backward_out[None])


def solution(mesh):
    in_specs = (
        P("section", "expert", None),
        P("section", "expert", None),
        P("section", "expert"),
        P("section", None),
        P("section", "expert", None, None),
        P("section", "expert", None, None),
        P("section", "expert", None, None),
        P("section", "expert", None),
        P("section", "expert", None),
        P("section", "expert"),
        P("section", "expert"),
    )
    out_specs = (P("section", "expert", None), P("section", "expert", None))
    return jax.shard_map(shards, mesh=mesh, in_specs=in_specs, out_specs=out_specs, check_vma=False)
```

```python
import jax
import jax.numpy as jnp
from jax import lax
from jax.experimental import pallas as pl
from jax.experimental.pallas import tpu as pltpu
from jax.sharding import PartitionSpec as P

EXPERTS = 8
CAP = 8
ROWS = 4
BLOCK = EXPERTS * CAP
EPSILON = 1e-06

FIRST = 1792
LAST = 1792
PART = 8
ACROSS = 1792
NEXT = ACROSS + 128
TOTAL = NEXT + 128
CHUNKS = ((0, 896), (896, 896), (FIRST, 896), (FIRST + 896, 896))
WIDTH = 256
HIDDEN = 128
VMEM_LIMIT = 40 * 1024 * 1024


def shift_section(block, distance):
    size = lax.axis_size("section")
    return lax.ppermute(block, "section", [((i - distance) % size, i) for i in range(size)])


def shift_y(block, distance):
    size = lax.axis_size("expert")
    route = [(k, k - k % ROWS + (k + distance) % ROWS) for k in range(size)]
    return lax.ppermute(block, "expert", route)


def swap_z(block):
    size = lax.axis_size("expert")
    return lax.ppermute(block, "expert", [(k, k ^ ROWS) for k in range(size)])


def exchange_z(block):
    groups = [[2 * ROWS * g + r for g in range(EXPERTS)] for r in range(2 * ROWS)]
    return lax.all_to_all(
        block, "expert", split_axis=0, concat_axis=0, axis_index_groups=groups, tiled=True
    )


def as_column(row):
    size = row.shape[1]
    down = lax.broadcasted_iota(jnp.int32, (size, size), 0)
    across = lax.broadcasted_iota(jnp.int32, (size, size), 1)
    spread = jnp.where(down == across, jnp.broadcast_to(row, (size, size)), 0.0)
    return jnp.sum(spread, axis=1, keepdims=True)


def pack_kernel(values, arrive, grad_back, send, table):
    features = arrive.shape[1]
    chosen = as_column(values[:, features : features + 128])
    weights = as_column(values[:, features + 128 : features + 256])
    shape = (2 * BLOCK, 2 * BLOCK)
    token = lax.broadcasted_iota(jnp.int32, shape, 0)
    column = lax.broadcasted_iota(jnp.int32, shape, 1)
    same = (column >> 4).astype(jnp.float32) == chosen
    same &= ((column >> 3) & 1) == (token >> 6)
    before = (column < token).astype(jnp.bfloat16)
    rank = mm(before, same.astype(jnp.bfloat16))
    onehot = (same & (rank == (column & 7).astype(jnp.float32))).astype(jnp.bfloat16)
    table[...] = onehot
    wide = arrive[...].astype(jnp.float32)
    inverse = lax.rsqrt(jnp.mean(wide * wide, axis=-1, keepdims=True) + EPSILON)
    normed = (wide * inverse * values[:, :features]).astype(jnp.bfloat16)
    scaled = (grad_back[...].astype(jnp.float32) * weights[BLOCK:]).astype(jnp.bfloat16)
    tokens = jnp.concatenate([normed, scaled], axis=0)
    send[...] = lax.dot_general(
        onehot, tokens, (((0,), (0,)), ((), ())), preferred_element_type=jnp.float32
    ).astype(send.dtype)


def finish_kernel(values, table, back, arrive, grad_back, forward_out, backward_out):
    features = arrive.shape[1]
    weights = as_column(values[:, features + 128 : features + 256])
    scales = as_column(values[:, features + 256 :])
    got = mm(table[...], back[...])
    wide = arrive[...].astype(jnp.float32)
    forward_out[...] = (wide + weights[:BLOCK] * got[:BLOCK]).astype(forward_out.dtype)
    back_wide = grad_back[...].astype(jnp.float32)
    grad_start = scales[BLOCK:] * values[:, :features] * got[BLOCK:]
    backward_out[...] = (back_wide + grad_start).astype(backward_out.dtype)


def gather_kernel(down_own, saved_across, saved_next, saved_previous, held_next, held_previous, sems):
    pieces = []
    for held, saved in ((held_next, saved_next), (held_previous, saved_previous)):
        pieces.append((saved_across, held.at[pl.ds(ACROSS, 128)]))
        pieces.append((saved, held.at[pl.ds(NEXT, 128)]))
        for c in range(down_own.shape[1] // WIDTH):
            block = down_own.at[:, pl.ds(c * WIDTH, WIDTH)]
            pieces.append((block, held.at[pl.ds(c * HIDDEN, HIDDEN)]))
    copies = [pltpu.make_async_copy(p[0], p[1], sems.at[i]) for i, p in enumerate(pieces)]
    for copy in copies:
        copy.start()
    for copy in copies:
        copy.wait()


def fetch(sources, buffers, sems):
    copies = [pltpu.make_async_copy(s, b, sems.at[i]) for i, (s, b) in enumerate(zip(sources, buffers))]
    for copy in copies:
        copy.start()
    return copies


def mm(a, b):
    return jnp.dot(a, b, preferred_element_type=jnp.float32)


def mt(a, b):
    return lax.dot_general(a, b, (((1,), (1,)), ((), ())), preferred_element_type=jnp.float32)


def activate(pre):
    gate, up = pre[:, :HIDDEN], pre[:, HIDDEN:]
    return (gate / (1.0 + jnp.exp(-gate)) * up).astype(jnp.bfloat16)


def factors(saved):
    wide = saved.astype(jnp.float32)
    gate, up = wide[:, :HIDDEN], wide[:, HIDDEN:]
    sigmoid = 1.0 / (1.0 + jnp.exp(-gate))
    return up * sigmoid * (1.0 + gate * (1.0 - sigmoid)), gate * sigmoid


def slope(grad_act, gate_factor, up_factor):
    return jnp.concatenate([grad_act * gate_factor, grad_act * up_factor], axis=1).astype(
        jnp.bfloat16
    )


def factor_kernel(own, behind, ahead, out):
    for i, saved in enumerate((own, behind, ahead)):
        rows = slice(i * 128, (i + 1) * 128)
        out[rows, :HIDDEN], out[rows, HIDDEN:] = factors(saved[...])


def down_blocks(held, start, count):
    return [held[start + c * HIDDEN : start + (c + 1) * HIDDEN] for c in range(count)]


def across_blocks(rows, held, start):
    count = rows.shape[1] // WIDTH
    total = 0.0
    for c, block in enumerate(down_blocks(held, start, count)):
        total = total + mt(rows[:, c * WIDTH : (c + 1) * WIDTH], block)
    return total


def near_kernel(rows_fwd, rows_bwd, factor, *refs):
    own_in, own_down, behind_in, behind, ahead_in, ahead, part, grad_part = refs
    count = rows_fwd.shape[1] // WIDTH

    def scaled(i, grad_act):
        rows = slice(i * 128, (i + 1) * 128)
        return slope(grad_act, factor[rows, :HIDDEN], factor[rows, HIDDEN:])

    acts = [activate(mm(rows_fwd[...], own_in[...]))]
    grads = [scaled(0, mt(rows_bwd[...], own_down[...]))]
    for i, near_in, near in ((1, behind_in, behind), (2, ahead_in, ahead)):
        acts.append(activate(mm(rows_fwd[...], near_in[...])))
        grads.append(scaled(i, across_blocks(rows_bwd, near, 0)))
    for c in range(count):
        columns = slice(c * WIDTH, (c + 1) * WIDTH)
        block = slice(c * HIDDEN, (c + 1) * HIDDEN)
        total = mm(acts[0], own_down[:, columns])
        part[:, columns] = total + mm(acts[1], behind[block]) + mm(acts[2], ahead[block])
    for start, size in CHUNKS:
        columns = slice(start, start + size)
        total = mt(grads[0], own_in[columns])
        total += mt(grads[1], behind_in[columns]) + mt(grads[2], ahead_in[columns])
        grad_part[:, columns] = total


def forward_kernel(rows, part, *refs):
    first, last, down_first, down_last, out = refs
    pre = mm(rows[:, :FIRST], first[...])
    act = activate(pre + mm(rows[:, FIRST:], last[...]))
    count = rows.shape[1] // WIDTH
    blocks = down_blocks(down_first, 0, PART) + down_blocks(down_last, 0, count - PART)
    for c, block in enumerate(blocks):
        columns = slice(c * WIDTH, (c + 1) * WIDTH)
        out[:, columns] = (part[:, columns] + mm(act, block)).astype(out.dtype)


def backward_kernel(rows, part, *refs):
    first, last, down_first, down_last, out = refs
    middle = PART * WIDTH
    grad_act = across_blocks(rows[:, :middle], down_first, 0)
    grad_act += across_blocks(rows[:, middle:], down_last, 0)
    grad = slope(grad_act, *factors(down_last[ACROSS - PART * HIDDEN :]))
    for start, size in CHUNKS:
        columns = slice(start, start + size)
        weights = first[columns] if start < FIRST else last[start - FIRST : start - FIRST + size]
        out[:, columns] = (part[:, columns] + mt(grad, weights)).astype(out.dtype)


def halves_kernel(behind, ahead, first, last, sems):
    one = pltpu.make_async_copy(behind.at[pl.ds(0, FIRST)], first, sems.at[0])
    two = pltpu.make_async_copy(ahead.at[pl.ds(FIRST, LAST)], last, sems.at[1])
    one.start()
    two.start()
    one.wait()
    two.wait()


def call(kernel, outs, whole, held=(), flops=0, traffic=8_000_000):
    in_vmem, left = pl.BlockSpec(memory_space=pltpu.VMEM), pl.BlockSpec(memory_space=pl.ANY)
    scratch = [pltpu.VMEM(h.shape, h.dtype) for h in held]
    scratch += [pltpu.SemaphoreType.DMA((len(held),))] if held else []
    return pl.pallas_call(
        kernel,
        out_shape=[jax.ShapeDtypeStruct(shape, dtype) for shape, dtype in outs],
        in_specs=[in_vmem] * len(whole) + [left] * len(held),
        out_specs=[in_vmem] * len(outs),
        scratch_shapes=scratch,
        compiler_params=pltpu.CompilerParams(vmem_limit_bytes=VMEM_LIMIT),
        cost_estimate=pl.CostEstimate(flops=flops, bytes_accessed=traffic, transcendentals=0),
    )(*whole, *held)


def shards(
    fwd_sent,
    grad_sent,
    saved_scale,
    norm_gain,
    w_in,
    w_down,
    saved_pre,
    route_fwd,
    route_bwd,
    weight_fwd,
    weight_bwd,
):
    features = fwd_sent.shape[2]
    place = lax.axis_index("expert")
    y = place % ROWS
    parity = (place // ROWS) % 2
    in_own, down_own = w_in[0, 0], w_down[0, 0]

    by_source = saved_pre[0, 0].reshape(EXPERTS, 2, ROWS, CAP, WIDTH)

    def saved_for(distance):
        column = lax.dynamic_index_in_dim(by_source, (y + distance) % ROWS, 2, keepdims=False)
        mine = lax.dynamic_index_in_dim(column, parity, 1, keepdims=False)
        other = lax.dynamic_index_in_dim(column, 1 - parity, 1, keepdims=False)
        return jnp.concatenate([mine, other]).reshape(-1, WIDTH)

    left = pl.BlockSpec(memory_space=pl.ANY)
    held_next, held_previous = pl.pallas_call(
        gather_kernel,
        out_shape=[jax.ShapeDtypeStruct((TOTAL, WIDTH), in_own.dtype)] * 2,
        in_specs=[left] * 4,
        out_specs=[pl.BlockSpec(memory_space=pltpu.VMEM)] * 2,
        scratch_shapes=[pltpu.SemaphoreType.DMA((4 + 2 * (features // WIDTH),))],
        cost_estimate=pl.CostEstimate(flops=0, bytes_accessed=2_000_000, transcendentals=0),
    )(down_own, saved_for(2), saved_for(1), saved_for(-1))
    behind_in, ahead_in = shift_y(in_own, 1), shift_y(in_own, -1)
    behind, ahead = shift_y(held_next, 1), shift_y(held_previous, -1)

    routes = [route.reshape(1, BLOCK).astype(jnp.float32) for route in (route_fwd, route_bwd)]
    values = jnp.concatenate(
        [norm_gain, *routes, weight_fwd, weight_bwd, saved_scale, saved_scale], axis=1
    )
    arrive = shift_section(fwd_sent[0], 1)
    grad_back = shift_section(grad_sent[0], -1)
    wide, narrow = (BLOCK, features), (2 * BLOCK, features)
    send, table = call(
        pack_kernel,
        [(narrow, jnp.bfloat16), ((2 * BLOCK, 2 * BLOCK), jnp.bfloat16)],
        (values, arrive, grad_back),
        flops=20_000_000_000,
    )
    own = exchange_z(send.reshape(EXPERTS, 2 * CAP, features))
    halves = pl.pallas_call(
        halves_kernel,
        out_shape=[jax.ShapeDtypeStruct((n, WIDTH), in_own.dtype) for n in (FIRST, LAST)],
        in_specs=[left] * 2,
        out_specs=[pl.BlockSpec(memory_space=pltpu.VMEM)] * 2,
        scratch_shapes=[pltpu.SemaphoreType.DMA((2,))],
        cost_estimate=pl.CostEstimate(flops=20_000_000_000, bytes_accessed=4_000_000, transcendentals=0),
    )(behind_in, ahead_in)
    far_in = (shift_y(halves[0], 1), shift_y(halves[1], -1))
    partner = swap_z(own)
    far_in, partner, saved_behind = lax.optimization_barrier(
        (far_in, partner, behind[NEXT:])
    )
    (factor,) = call(
        factor_kernel,
        [((384, WIDTH), jnp.float32)],
        (saved_for(0), saved_behind, ahead[NEXT:]),
        flops=1_000_000_000,
    )
    far_down = (
        shift_y(behind[: PART * HIDDEN], 1),
        shift_y(ahead[PART * HIDDEN : NEXT], -1),
    )
    far = (*far_in, *far_down)
    rows = jnp.stack([own, partner]).reshape(2 * EXPERTS, 2, CAP, features)
    rows_fwd = rows[:, 0].reshape(-1, features)
    rows_bwd = rows[:, 1].reshape(-1, features)

    part, grad_part = call(
        near_kernel,
        [(narrow, jnp.float32)] * 2,
        (rows_fwd, rows_bwd, factor, in_own, down_own, behind_in, behind, ahead_in, ahead),
        flops=2_000_000_000,
        traffic=0,
    )
    (part,) = call(forward_kernel, [(narrow, jnp.bfloat16)], (rows_fwd, part, *far), flops=350_000_000)
    received_fwd = swap_z(part[BLOCK:])
    (grad_part,) = call(backward_kernel, [(narrow, jnp.bfloat16)], (rows_bwd, grad_part, *far), flops=350_000_000)
    received_bwd = swap_z(grad_part[BLOCK:])

    def add(product, received):
        total = product[:BLOCK].astype(jnp.float32) + received.astype(jnp.float32)
        return total.astype(jnp.bfloat16).reshape(EXPERTS, CAP, features)

    sums = [add(part, received_fwd), add(grad_part, received_bwd)]
    back = exchange_z(jnp.concatenate(sums, axis=1)).reshape(narrow)
    forward_out, backward_out = call(
        finish_kernel,
        [(wide, jnp.bfloat16)] * 2,
        (values, table, back, arrive, grad_back),
    )
    return (forward_out[None], backward_out[None])


def solution(mesh):
    in_specs = (
        P("section", "expert", None),
        P("section", "expert", None),
        P("section", "expert"),
        P("section", None),
        P("section", "expert", None, None),
        P("section", "expert", None, None),
        P("section", "expert", None, None),
        P("section", "expert", None),
        P("section", "expert", None),
        P("section", "expert"),
        P("section", "expert"),
    )
    out_specs = (P("section", "expert", None), P("section", "expert", None))
    return jax.shard_map(shards, mesh=mesh, in_specs=in_specs, out_specs=out_specs, check_vma=False)
```

```python
import jax
import jax.numpy as jnp
from jax import lax
from jax.experimental import pallas as pl
from jax.experimental.pallas import tpu as pltpu
from jax.sharding import PartitionSpec as P

EXPERTS = 8
CAP = 8
ROWS = 4
BLOCK = EXPERTS * CAP
EPSILON = 1e-06

FIRST = 1792
LAST = 1792
PART = 8
ACROSS = 1792
NEXT = ACROSS + 128
TOTAL = NEXT + 128
CHUNKS = ((0, 896), (896, 896), (FIRST, 896), (FIRST + 896, 896))
WIDTH = 256
HIDDEN = 128
VMEM_LIMIT = 40 * 1024 * 1024


def shift_section(block, distance):
    size = lax.axis_size("section")
    return lax.ppermute(block, "section", [((i - distance) % size, i) for i in range(size)])


def shift_y(block, distance):
    size = lax.axis_size("expert")
    route = [(k, k - k % ROWS + (k + distance) % ROWS) for k in range(size)]
    return lax.ppermute(block, "expert", route)


def swap_z(block):
    size = lax.axis_size("expert")
    return lax.ppermute(block, "expert", [(k, k ^ ROWS) for k in range(size)])


def exchange_z(block):
    groups = [[2 * ROWS * g + r for g in range(EXPERTS)] for r in range(2 * ROWS)]
    return lax.all_to_all(
        block, "expert", split_axis=0, concat_axis=0, axis_index_groups=groups, tiled=True
    )


def as_column(row):
    size = row.shape[1]
    down = lax.broadcasted_iota(jnp.int32, (size, size), 0)
    across = lax.broadcasted_iota(jnp.int32, (size, size), 1)
    spread = jnp.where(down == across, jnp.broadcast_to(row, (size, size)), 0.0)
    return jnp.sum(spread, axis=1, keepdims=True)


def pack_kernel(values, arrive, grad_back, send, table):
    features = arrive.shape[1]
    chosen = as_column(values[:, features : features + 128])
    weights = as_column(values[:, features + 128 : features + 256])
    shape = (2 * BLOCK, 2 * BLOCK)
    token = lax.broadcasted_iota(jnp.int32, shape, 0)
    column = lax.broadcasted_iota(jnp.int32, shape, 1)
    same = (column >> 4).astype(jnp.float32) == chosen
    same &= ((column >> 3) & 1) == (token >> 6)
    before = (column < token).astype(jnp.bfloat16)
    rank = mm(before, same.astype(jnp.bfloat16))
    onehot = (same & (rank == (column & 7).astype(jnp.float32))).astype(jnp.bfloat16)
    table[...] = onehot
    wide = arrive[...].astype(jnp.float32)
    inverse = lax.rsqrt(jnp.mean(wide * wide, axis=-1, keepdims=True) + EPSILON)
    normed = (wide * inverse * values[:, :features]).astype(jnp.bfloat16)
    scaled = (grad_back[...].astype(jnp.float32) * weights[BLOCK:]).astype(jnp.bfloat16)
    tokens = jnp.concatenate([normed, scaled], axis=0)
    send[...] = lax.dot_general(
        onehot, tokens, (((0,), (0,)), ((), ())), preferred_element_type=jnp.float32
    ).astype(send.dtype)


def finish_kernel(values, table, back, arrive, grad_back, forward_out, backward_out):
    features = arrive.shape[1]
    weights = as_column(values[:, features + 128 : features + 256])
    scales = as_column(values[:, features + 256 :])
    got = mm(table[...], back[...])
    wide = arrive[...].astype(jnp.float32)
    forward_out[...] = (wide + weights[:BLOCK] * got[:BLOCK]).astype(forward_out.dtype)
    back_wide = grad_back[...].astype(jnp.float32)
    grad_start = scales[BLOCK:] * values[:, :features] * got[BLOCK:]
    backward_out[...] = (back_wide + grad_start).astype(backward_out.dtype)


def gather_kernel(down_own, saved_across, saved_next, saved_previous, held_next, held_previous, sems):
    pieces = []
    for held, saved in ((held_next, saved_next), (held_previous, saved_previous)):
        pieces.append((saved_across, held.at[pl.ds(ACROSS, 128)]))
        pieces.append((saved, held.at[pl.ds(NEXT, 128)]))
        for c in range(down_own.shape[1] // WIDTH):
            block = down_own.at[:, pl.ds(c * WIDTH, WIDTH)]
            pieces.append((block, held.at[pl.ds(c * HIDDEN, HIDDEN)]))
    copies = [pltpu.make_async_copy(p[0], p[1], sems.at[i]) for i, p in enumerate(pieces)]
    for copy in copies:
        copy.start()
    for copy in copies:
        copy.wait()


def fetch(sources, buffers, sems):
    copies = [pltpu.make_async_copy(s, b, sems.at[i]) for i, (s, b) in enumerate(zip(sources, buffers))]
    for copy in copies:
        copy.start()
    return copies


def mm(a, b):
    return jnp.dot(a, b, preferred_element_type=jnp.float32)


def mt(a, b):
    return lax.dot_general(a, b, (((1,), (1,)), ((), ())), preferred_element_type=jnp.float32)


def activate(pre):
    gate, up = pre[:, :HIDDEN], pre[:, HIDDEN:]
    return (gate / (1.0 + jnp.exp(-gate)) * up).astype(jnp.bfloat16)


def factors(saved):
    wide = saved.astype(jnp.float32)
    gate, up = wide[:, :HIDDEN], wide[:, HIDDEN:]
    sigmoid = 1.0 / (1.0 + jnp.exp(-gate))
    return up * sigmoid * (1.0 + gate * (1.0 - sigmoid)), gate * sigmoid


def slope(grad_act, gate_factor, up_factor):
    return jnp.concatenate([grad_act * gate_factor, grad_act * up_factor], axis=1).astype(
        jnp.bfloat16
    )


def factor_kernel(own, behind, ahead, out):
    for i, saved in enumerate((own, behind, ahead)):
        rows = slice(i * 128, (i + 1) * 128)
        out[rows, :HIDDEN], out[rows, HIDDEN:] = factors(saved[...])


def down_blocks(held, start, count):
    return [held[start + c * HIDDEN : start + (c + 1) * HIDDEN] for c in range(count)]


def across_blocks(rows, held, start):
    count = rows.shape[1] // WIDTH
    total = 0.0
    for c, block in enumerate(down_blocks(held, start, count)):
        total = total + mt(rows[:, c * WIDTH : (c + 1) * WIDTH], block)
    return total


def near_kernel(rows_fwd, rows_bwd, factor, *refs):
    own_in, own_down, behind_in, behind, ahead_in, ahead, part, grad_part = refs
    count = rows_fwd.shape[1] // WIDTH

    def scaled(i, grad_act):
        rows = slice(i * 128, (i + 1) * 128)
        return slope(grad_act, factor[rows, :HIDDEN], factor[rows, HIDDEN:])

    acts = [activate(mm(rows_fwd[...], own_in[...]))]
    grads = [scaled(0, mt(rows_bwd[...], own_down[...]))]
    for i, near_in, near in ((1, behind_in, behind), (2, ahead_in, ahead)):
        acts.append(activate(mm(rows_fwd[...], near_in[...])))
        grads.append(scaled(i, across_blocks(rows_bwd, near, 0)))
    both = jnp.concatenate(acts[1:], axis=1)
    for c in range(count):
        columns = slice(c * WIDTH, (c + 1) * WIDTH)
        block = slice(c * HIDDEN, (c + 1) * HIDDEN)
        total = mm(acts[0], own_down[:, columns])
        part[:, columns] = total + mm(both, jnp.concatenate([behind[block], ahead[block]], axis=0))
    for start, size in CHUNKS:
        columns = slice(start, start + size)
        total = mt(grads[0], own_in[columns])
        total += mt(grads[1], behind_in[columns]) + mt(grads[2], ahead_in[columns])
        grad_part[:, columns] = total


def forward_kernel(rows, part, *refs):
    first, last, down_first, down_last, out = refs
    pre = mm(rows[:, :FIRST], first[...])
    act = activate(pre + mm(rows[:, FIRST:], last[...]))
    count = rows.shape[1] // WIDTH
    blocks = down_blocks(down_first, 0, PART) + down_blocks(down_last, 0, count - PART)
    for c, block in enumerate(blocks):
        columns = slice(c * WIDTH, (c + 1) * WIDTH)
        out[:, columns] = (part[:, columns] + mm(act, block)).astype(out.dtype)


def backward_kernel(rows, part, *refs):
    first, last, down_first, down_last, out = refs
    middle = PART * WIDTH
    grad_act = across_blocks(rows[:, :middle], down_first, 0)
    grad_act += across_blocks(rows[:, middle:], down_last, 0)
    grad = slope(grad_act, *factors(down_last[ACROSS - PART * HIDDEN :]))
    for start, size in CHUNKS:
        columns = slice(start, start + size)
        weights = first[columns] if start < FIRST else last[start - FIRST : start - FIRST + size]
        out[:, columns] = (part[:, columns] + mt(grad, weights)).astype(out.dtype)


def halves_kernel(behind, ahead, first, last, sems):
    one = pltpu.make_async_copy(behind.at[pl.ds(0, FIRST)], first, sems.at[0])
    two = pltpu.make_async_copy(ahead.at[pl.ds(FIRST, LAST)], last, sems.at[1])
    one.start()
    two.start()
    one.wait()
    two.wait()


def call(kernel, outs, whole, held=(), flops=0, traffic=8_000_000):
    in_vmem, left = pl.BlockSpec(memory_space=pltpu.VMEM), pl.BlockSpec(memory_space=pl.ANY)
    scratch = [pltpu.VMEM(h.shape, h.dtype) for h in held]
    scratch += [pltpu.SemaphoreType.DMA((len(held),))] if held else []
    return pl.pallas_call(
        kernel,
        out_shape=[jax.ShapeDtypeStruct(shape, dtype) for shape, dtype in outs],
        in_specs=[in_vmem] * len(whole) + [left] * len(held),
        out_specs=[in_vmem] * len(outs),
        scratch_shapes=scratch,
        compiler_params=pltpu.CompilerParams(vmem_limit_bytes=VMEM_LIMIT),
        cost_estimate=pl.CostEstimate(flops=flops, bytes_accessed=traffic, transcendentals=0),
    )(*whole, *held)


def shards(
    fwd_sent,
    grad_sent,
    saved_scale,
    norm_gain,
    w_in,
    w_down,
    saved_pre,
    route_fwd,
    route_bwd,
    weight_fwd,
    weight_bwd,
):
    features = fwd_sent.shape[2]
    place = lax.axis_index("expert")
    y = place % ROWS
    parity = (place // ROWS) % 2
    in_own, down_own = w_in[0, 0], w_down[0, 0]

    by_source = saved_pre[0, 0].reshape(EXPERTS, 2, ROWS, CAP, WIDTH)

    def saved_for(distance):
        column = lax.dynamic_index_in_dim(by_source, (y + distance) % ROWS, 2, keepdims=False)
        mine = lax.dynamic_index_in_dim(column, parity, 1, keepdims=False)
        other = lax.dynamic_index_in_dim(column, 1 - parity, 1, keepdims=False)
        return jnp.concatenate([mine, other]).reshape(-1, WIDTH)

    left = pl.BlockSpec(memory_space=pl.ANY)
    held_next, held_previous = pl.pallas_call(
        gather_kernel,
        out_shape=[jax.ShapeDtypeStruct((TOTAL, WIDTH), in_own.dtype)] * 2,
        in_specs=[left] * 4,
        out_specs=[pl.BlockSpec(memory_space=pltpu.VMEM)] * 2,
        scratch_shapes=[pltpu.SemaphoreType.DMA((4 + 2 * (features // WIDTH),))],
        cost_estimate=pl.CostEstimate(flops=0, bytes_accessed=2_000_000, transcendentals=0),
    )(down_own, saved_for(2), saved_for(1), saved_for(-1))
    behind_in, ahead_in = shift_y(in_own, 1), shift_y(in_own, -1)
    behind, ahead = shift_y(held_next, 1), shift_y(held_previous, -1)

    routes = [route.reshape(1, BLOCK).astype(jnp.float32) for route in (route_fwd, route_bwd)]
    values = jnp.concatenate(
        [norm_gain, *routes, weight_fwd, weight_bwd, saved_scale, saved_scale], axis=1
    )
    arrive = shift_section(fwd_sent[0], 1)
    grad_back = shift_section(grad_sent[0], -1)
    wide, narrow = (BLOCK, features), (2 * BLOCK, features)
    send, table = call(
        pack_kernel,
        [(narrow, jnp.bfloat16), ((2 * BLOCK, 2 * BLOCK), jnp.bfloat16)],
        (values, arrive, grad_back),
        flops=20_000_000_000,
    )
    own = exchange_z(send.reshape(EXPERTS, 2 * CAP, features))
    halves = pl.pallas_call(
        halves_kernel,
        out_shape=[jax.ShapeDtypeStruct((n, WIDTH), in_own.dtype) for n in (FIRST, LAST)],
        in_specs=[left] * 2,
        out_specs=[pl.BlockSpec(memory_space=pltpu.VMEM)] * 2,
        scratch_shapes=[pltpu.SemaphoreType.DMA((2,))],
        cost_estimate=pl.CostEstimate(flops=20_000_000_000, bytes_accessed=4_000_000, transcendentals=0),
    )(behind_in, ahead_in)
    far_in = (shift_y(halves[0], 1), shift_y(halves[1], -1))
    partner = swap_z(own)
    far_in, partner, saved_behind = lax.optimization_barrier(
        (far_in, partner, behind[NEXT:])
    )
    (factor,) = call(
        factor_kernel,
        [((384, WIDTH), jnp.float32)],
        (saved_for(0), saved_behind, ahead[NEXT:]),
        flops=1_000_000_000,
    )
    far_down = (
        shift_y(behind[: PART * HIDDEN], 1),
        shift_y(ahead[PART * HIDDEN : NEXT], -1),
    )
    far = (*far_in, *far_down)
    rows = jnp.stack([own, partner]).reshape(2 * EXPERTS, 2, CAP, features)
    rows_fwd = rows[:, 0].reshape(-1, features)
    rows_bwd = rows[:, 1].reshape(-1, features)

    part, grad_part = call(
        near_kernel,
        [(narrow, jnp.float32)] * 2,
        (rows_fwd, rows_bwd, factor, in_own, down_own, behind_in, behind, ahead_in, ahead),
        flops=2_000_000_000,
        traffic=0,
    )
    (part,) = call(forward_kernel, [(narrow, jnp.bfloat16)], (rows_fwd, part, *far), flops=350_000_000)
    received_fwd = swap_z(part[BLOCK:])
    (grad_part,) = call(backward_kernel, [(narrow, jnp.bfloat16)], (rows_bwd, grad_part, *far), flops=350_000_000)
    received_bwd = swap_z(grad_part[BLOCK:])

    def add(product, received):
        total = product[:BLOCK].astype(jnp.float32) + received.astype(jnp.float32)
        return total.astype(jnp.bfloat16).reshape(EXPERTS, CAP, features)

    sums = [add(part, received_fwd), add(grad_part, received_bwd)]
    back = exchange_z(jnp.concatenate(sums, axis=1)).reshape(narrow)
    forward_out, backward_out = call(
        finish_kernel,
        [(wide, jnp.bfloat16)] * 2,
        (values, table, back, arrive, grad_back),
    )
    return (forward_out[None], backward_out[None])


def solution(mesh):
    in_specs = (
        P("section", "expert", None),
        P("section", "expert", None),
        P("section", "expert"),
        P("section", None),
        P("section", "expert", None, None),
        P("section", "expert", None, None),
        P("section", "expert", None, None),
        P("section", "expert", None),
        P("section", "expert", None),
        P("section", "expert"),
        P("section", "expert"),
    )
    out_specs = (P("section", "expert", None), P("section", "expert", None))
    return jax.shard_map(shards, mesh=mesh, in_specs=in_specs, out_specs=out_specs, check_vma=False)
```
